32 devices in a mesh: ia: 4 (over z), ja: 4 (over y, x), ka: 2 (over core).
Axes of the slice: x: 2, y: 2, z: 4, core: 2. Of those that a mesh axis runs over, the one named last changes fastest.
Arguments:
- tensor: float32 [1024, 1024, 512], P('ia', 'ja', 'ka'), may hold values from -6 to 6
- factor_first: float32 [1024, 32], P(('ia', 'ja', 'ka')), may hold values from -0.75 to 0.75
- factor_second: float32 [1024, 32], P(('ja', 'ia', 'ka')), may hold values from -0.375 to 0.375
- factor_third: float32 [512, 32], P(('ka', 'ia', 'ja')), may hold values from -0.375 to 0.375
Outputs:
- gradient: float32 [1024, 32], P(('ia', 'ja', 'ka'))
The draws below stay inside these ranges and needn't reach their ends.
All inputs are finite; a program needn't handle non-finite values.
Results may differ from the reference program's by a relative error of at most 0.000082.
Values sent between devices are 32-bit elements; how exact they have to be, the bound alone decides.
A program may use at most 128 MiB of HBM per device.

```python
import jax
import jax.numpy as jnp
from jax import lax

I = 1024
J = 1024
K = 512
R = 32


def strengthened(result, stream_key, source, target, shards_of, factor):
    owner, partner = [(jnp.arange(result.shape[axis_at]) // (result.shape[axis_at] // shards_of)).reshape([-1 if axis == axis_at else 1 for axis in range(result.ndim)]) for axis_at in (source, target)]
    chosen = jax.random.permutation(stream_key, shards_of)[partner]
    strong = (owner == chosen) | (owner == (partner + shards_of // 2) % shards_of)
    return jnp.where(strong, factor * result, result)


def block_scale(stream_key, extent, cuts, least, top_value):
    factor_of = 1.0
    for position, parts in cuts:
        heights = jax.random.uniform(jax.random.fold_in(jax.random.fold_in(stream_key, 6), position), (parts,), jnp.float32, least / len(cuts), top_value / len(cuts))
        factor_of = factor_of * jnp.repeat(jnp.exp(heights), extent[position] // parts).reshape((-1,) + (1,) * (len(extent) - 1 - position))
    return factor_of


def normal_values(stream_key, shape, deviation, limit, split=(), dtype=jnp.bfloat16):
    drawn = jax.random.normal(stream_key, shape, jnp.float32) * deviation
    if len(split) > 0:
        drawn = block_scale(stream_key, shape, split, -0.22, 0.18) * drawn
    return jnp.clip(drawn, min=-limit, max=limit).astype(dtype)


def noise_with(own_key, shape, deviation, bound, pieces, heavy, kind=jnp.bfloat16):
    drawn = deviation * jax.random.normal(own_key, shape, jnp.float32)
    if pieces:
        drawn = drawn * block_scale(own_key, shape, pieces, -0.22, 0.18)
    return jnp.clip(strengthened(drawn, jax.random.fold_in(own_key, 3), *heavy), -bound, bound).astype(kind)


def setup_inputs(seed: int = 0) -> dict:
    seeds = jax.random.split(jax.random.key(seed), 5)
    return {
        "tensor": noise_with(seeds[0], (I, J, K), 1.0, 6.0, ((0, 4), (1, 4), (2, 2)), (1, 0, 4, 2.0), jnp.float32),
        "factor_first": normal_values(seeds[1], (I, R), 0.125, 0.75, ((0, 32),), jnp.float32),
        "factor_second": normal_values(seeds[2], (J, R), 0.0625, 0.375, ((0, 32),), jnp.float32),
        "factor_third": normal_values(seeds[3], (K, R), 0.0625, 0.375, ((0, 32),), jnp.float32),
    }


def reference(tensor, factor_first, factor_second, factor_third):
    blocks = tensor.reshape(I // 64, 64, J, K)

    def one_block(block):
        partial_value = jnp.einsum("ijk,kr->ijr", block, factor_third, precision=lax.Precision.HIGHEST)
        return jnp.einsum("ijr,jr->ir", partial_value, factor_second, precision=lax.Precision.HIGHEST)

    product = lax.map(one_block, blocks).reshape(I, R)
    gram_second = jnp.dot(factor_second.T, factor_second, precision=lax.Precision.HIGHEST)
    gram_third = jnp.dot(factor_third.T, factor_third, precision=lax.Precision.HIGHEST)
    return jnp.dot(factor_first, gram_second * gram_third, precision=lax.Precision.HIGHEST) - product
```

```python
import functools

import jax
import jax.numpy as jnp
from jax import lax
from jax.experimental import pallas as pl
from jax.experimental.pallas import tpu as pltpu
from jax.sharding import PartitionSpec as P

MESH = pl.DeviceIdType.MESH
HIGHEST = lax.Precision.HIGHEST
TOGETHER = 2
CHUNK_ROWS = 8
BUFFERS = 20
EARLY = 8


def split(x):
    high = x.astype(jnp.bfloat16)
    low = (x - high.astype(jnp.float32)).astype(jnp.bfloat16)
    return high, low


def kernel(
    na, nj, nk, chunk_rows, buffers,
    x_hbm, first_ref, second_ref, third_ref, out_ref,
    x_buf, x_sem,
    third_all, third_send, third_recv,
    second_all, second_send, second_recv,
    third_flat, second_flat, weights, scale,
    gram3, gram3_send, gram3_recv,
    gram2, gram2_send, gram2_recv,
    part, terms_out, terms_in, term_send, term_recv,
):
    ia, ja, ka = lax.axis_index("ia"), lax.axis_index("ja"), lax.axis_index("ka")
    n_owner = nj * nk
    own = ja * nk + ka
    rows = out_ref.shape[0]
    rank = out_ref.shape[1]
    per_owner = rows // chunk_rows
    chunks = n_owner * per_owner

    def owner_at(turn):
        return lax.rem(own + 1 + turn, n_owner)

    def x_copy(c):
        start = owner_at(c // per_owner) * rows + lax.rem(c, per_owner) * chunk_rows
        slot = lax.rem(c, buffers)
        return pltpu.make_async_copy(
            x_hbm.at[pl.ds(start, chunk_rows)], x_buf.at[slot], x_sem.at[slot]
        )

    def start_x(c, carry):
        x_copy(c).start()
        return carry

    early = min(EARLY, buffers)
    lax.fori_loop(0, early, start_x, 0)

    def third_peer(d):
        at = lax.rem(ia * nj + ja + d, na * nj)
        return at // nj, lax.rem(at, nj)

    def second_peer(d):
        at = lax.rem(ia * nk + ka + d, na * nk)
        return at // nk, lax.rem(at, nk)

    barrier = pltpu.get_barrier_semaphore()

    def greet(device):
        pl.semaphore_signal(barrier, inc=1, device_id=device, device_id_type=MESH)

    def greet_third(d, carry):
        pa, pj = third_peer(d)
        greet((pa, pj, ka))
        return carry

    lax.fori_loop(1, na * nj, greet_third, 0)
    for dk in range(1, nk):
        pk = lax.rem(ka + dk, nk)
        for da in range(na):
            greet((lax.rem(ia + da, na), ja, pk))
        for dj in range(1, nj):
            greet((ia, lax.rem(ja + dj, nj), pk))
    pl.semaphore_wait(barrier, na * nj - 1 + (nk - 1) * (na + nj - 1))

    third_at = ia * nj + ja
    second_at = ia * nk + ka

    def third_copy(d):
        pa, pj = third_peer(d)
        return pltpu.make_async_remote_copy(
            src_ref=third_ref, dst_ref=third_all.at[third_at],
            send_sem=third_send.at[d], recv_sem=third_recv.at[third_at],
            device_id=(pa, pj, ka), device_id_type=MESH,
        )

    def second_copy(d):
        pa, pk = second_peer(d)
        return pltpu.make_async_remote_copy(
            src_ref=second_ref, dst_ref=second_all.at[second_at],
            send_sem=second_send.at[d], recv_sem=second_recv.at[second_at],
            device_id=(pa, ja, pk), device_id_type=MESH,
        )

    def start_third(d, carry):
        third_copy(d).start()
        return carry

    def start_second(d, carry):
        second_copy(d).start()
        return carry

    lax.fori_loop(1, na * nj, start_third, 0)
    lax.fori_loop(1, na * nk, start_second, 0)
    lax.fori_loop(early, buffers, start_x, 0)
    third_all[third_at] = third_ref[...]
    second_all[second_at] = second_ref[...]

    def recv_third(d, carry):
        pa, pj = third_peer(d)
        at = pa * nj + pj
        pltpu.make_async_remote_copy(
            src_ref=third_ref, dst_ref=third_all.at[at],
            send_sem=third_send.at[d], recv_sem=third_recv.at[at],
            device_id=(pa, pj, ka), device_id_type=MESH,
        ).wait_recv()
        return carry

    def recv_second(d, carry):
        pa, pk = second_peer(d)
        at = pa * nk + pk
        pltpu.make_async_remote_copy(
            src_ref=second_ref, dst_ref=second_all.at[at],
            send_sem=second_send.at[d], recv_sem=second_recv.at[at],
            device_id=(pa, ja, pk), device_id_type=MESH,
        ).wait_recv()
        return carry

    lax.fori_loop(1, na * nj, recv_third, 0)
    lax.fori_loop(1, na * nk, recv_second, 0)

    depth = third_ref.shape[0]
    for s in range(na * nj):
        third_flat[s * depth:(s + 1) * depth, :] = third_all[s]
    width = second_ref.shape[0]
    for s in range(na * nk):
        second_flat[s * width:(s + 1) * width, :] = second_all[s]

    third = third_flat[...]
    second = second_flat[...]
    high, low = split(third)
    both = jnp.concatenate([high, low], axis=1)
    weights[...] = jnp.concatenate([both, both], axis=0)
    scale[...] = jnp.concatenate([second, second], axis=1)

    over_rows = (((0,), (0,)), ((), ()))
    gram3[ka] = lax.dot_general(
        third, third, over_rows, precision=HIGHEST, preferred_element_type=jnp.float32
    )
    gram2[ja] = lax.dot_general(
        second, second, over_rows, precision=HIGHEST, preferred_element_type=jnp.float32
    )

    def gram3_copy(d, at):
        return pltpu.make_async_remote_copy(
            src_ref=gram3.at[at], dst_ref=gram3.at[at],
            send_sem=gram3_send.at[d], recv_sem=gram3_recv.at[at],
            device_id=(ia, ja, lax.rem(ka + d, nk)), device_id_type=MESH,
        )

    def gram2_copy(d, at):
        return pltpu.make_async_remote_copy(
            src_ref=gram2.at[at], dst_ref=gram2.at[at],
            send_sem=gram2_send.at[d], recv_sem=gram2_recv.at[at],
            device_id=(ia, lax.rem(ja + d, nj), ka), device_id_type=MESH,
        )

    for d in range(1, nk):
        gram3_copy(d, ka).start()
    for d in range(1, nj):
        gram2_copy(d, ja).start()

    columns = x_hbm.shape[1]
    inner = x_hbm.shape[2]
    together = min(TOGETHER, chunk_rows)

    def chunk(c, carry):
        slot = lax.rem(c, buffers)
        x_copy(c).wait()
        base = lax.rem(c, per_owner) * chunk_rows

        def few(g, carry):
            i = g * together
            x = x_buf[slot, pl.ds(i, together)].reshape(together * columns, inner)
            high, low = split(x)
            y = jnp.dot(
                jnp.concatenate([high, low], axis=1), weights[...],
                preferred_element_type=jnp.float32,
            )
            y = y.reshape(together, columns // 8, 8, 2 * rank)
            y = y * scale[...].reshape(columns // 8, 8, 2 * rank)[None]
            part[pl.ds(base + i, together)] = jnp.sum(y, axis=1)
            return carry

        lax.fori_loop(0, chunk_rows // together, few, 0)

        @pl.when(c + buffers < chunks)
        def _():
            x_copy(c + buffers).start()

        return carry

    def term():
        both = jnp.sum(part[...], axis=1)
        return both[:, :rank] + both[:, rank:]

    def term_copy(turn):
        owner = owner_at(turn)
        return pltpu.make_async_remote_copy(
            src_ref=terms_out.at[turn], dst_ref=terms_in.at[own],
            send_sem=term_send.at[turn], recv_sem=term_recv.at[own],
            device_id=(ia, owner // nk, lax.rem(owner, nk)), device_id_type=MESH,
        )

    def for_other(turn, carry):
        lax.fori_loop(turn * per_owner, (turn + 1) * per_owner, chunk, 0)
        terms_out[turn] = term()
        term_copy(turn).start()
        return carry

    lax.fori_loop(0, n_owner - 1, for_other, 0)
    lax.fori_loop((n_owner - 1) * per_owner, n_owner * per_owner, chunk, 0)
    terms_in[own] = term()

    for d in range(1, nk):
        gram3_copy(d, lax.rem(ka + d, nk)).wait_recv()
    for d in range(1, nj):
        gram2_copy(d, lax.rem(ja + d, nj)).wait_recv()
    mixed = jnp.sum(gram2[...], axis=0) * jnp.sum(gram3[...], axis=0)
    gradient = jnp.dot(
        first_ref[...], mixed, precision=HIGHEST, preferred_element_type=jnp.float32
    )

    def recv_term(turn, carry):
        owner = owner_at(turn)
        pltpu.make_async_remote_copy(
            src_ref=terms_out.at[turn], dst_ref=terms_in.at[owner],
            send_sem=term_send.at[turn], recv_sem=term_recv.at[owner],
            device_id=(ia, owner // nk, lax.rem(owner, nk)), device_id_type=MESH,
        ).wait_recv()
        return carry

    lax.fori_loop(0, n_owner - 1, recv_term, 0)
    out_ref[...] = gradient - jnp.sum(terms_in[...], axis=0)

    def sent_third(d, carry):
        third_copy(d).wait_send()
        return carry

    def sent_second(d, carry):
        second_copy(d).wait_send()
        return carry

    def sent_term(turn, carry):
        term_copy(turn).wait_send()
        return carry

    lax.fori_loop(1, na * nj, sent_third, 0)
    lax.fori_loop(1, na * nk, sent_second, 0)
    for d in range(1, nk):
        gram3_copy(d, ka).wait_send()
    for d in range(1, nj):
        gram2_copy(d, ja).wait_send()
    lax.fori_loop(0, n_owner - 1, sent_term, 0)


def on_device(na, nj, nk, tensor, first, second, third):
    rows, rank = first.shape
    _, columns, inner = tensor.shape
    chunk_rows = min(CHUNK_ROWS, rows)
    buffers = min(BUFFERS, nj * nk * (rows // chunk_rows))
    dma = pltpu.SemaphoreType.DMA
    f32 = jnp.float32
    vmem = pl.BlockSpec(memory_space=pltpu.VMEM)
    return pl.pallas_call(
        functools.partial(kernel, na, nj, nk, chunk_rows, buffers),
        out_shape=jax.ShapeDtypeStruct((rows, rank), f32),
        in_specs=[pl.BlockSpec(memory_space=pl.ANY), vmem, vmem, vmem],
        out_specs=vmem,
        scratch_shapes=[
            pltpu.VMEM((buffers, chunk_rows, columns, inner), f32),
            dma((buffers,)),
            pltpu.VMEM((na * nj,) + third.shape, f32),
            dma((na * nj,)),
            dma((na * nj,)),
            pltpu.VMEM((na * nk,) + second.shape, f32),
            dma((na * nk,)),
            dma((na * nk,)),
            pltpu.VMEM((inner, rank), f32),
            pltpu.VMEM((columns, rank), f32),
            pltpu.VMEM((2 * inner, 2 * rank), jnp.bfloat16),
            pltpu.VMEM((columns, 2 * rank), f32),
            pltpu.VMEM((nk, rank, rank), f32),
            dma((nk,)),
            dma((nk,)),
            pltpu.VMEM((nj, rank, rank), f32),
            dma((nj,)),
            dma((nj,)),
            pltpu.VMEM((rows, 8, 2 * rank), f32),
            pltpu.VMEM((nj * nk, rows, rank), f32),
            pltpu.VMEM((nj * nk, rows, rank), f32),
            dma((nj * nk,)),
            dma((nj * nk,)),
        ],
        compiler_params=pltpu.CompilerParams(
            collective_id=0, has_side_effects=True, vmem_limit_bytes=56 * 2**20
        ),
        name="cp_gradient",
    )(tensor, first, second, third)


def solution(mesh):
    sizes = (mesh.shape["ia"], mesh.shape["ja"], mesh.shape["ka"])
    return jax.shard_map(
        functools.partial(on_device, *sizes),
        mesh=mesh,
        in_specs=(
            P("ia", "ja", "ka"),
            P(("ia", "ja", "ka"), None),
            P(("ja", "ia", "ka"), None),
            P(("ka", "ia", "ja"), None),
        ),
        out_specs=P(("ia", "ja", "ka"), None),
        check_vma=False,
    )
```

```python
import functools

import jax
import jax.numpy as jnp
from jax import lax
from jax.experimental import pallas as pl
from jax.experimental.pallas import tpu as pltpu
from jax.sharding import PartitionSpec as P

MESH = pl.DeviceIdType.MESH
HIGHEST = lax.Precision.HIGHEST
TOGETHER = 8
CHUNK_ROWS = 8
BUFFERS = 20
EARLY = 8


def split(x):
    high = x.astype(jnp.bfloat16)
    low = (x - high.astype(jnp.float32)).astype(jnp.bfloat16)
    return high, low


def kernel(
    na, nj, nk, chunk_rows, buffers,
    x_hbm, first_ref, second_ref, third_ref, out_ref,
    x_buf, x_sem,
    third_all, third_send, third_recv,
    second_all, second_send, second_recv,
    third_flat, second_flat, weights, scale,
    gram3, gram3_send, gram3_recv,
    gram2, gram2_send, gram2_recv,
    part, terms_out, terms_in, term_send, term_recv,
):
    ia, ja, ka = lax.axis_index("ia"), lax.axis_index("ja"), lax.axis_index("ka")
    n_owner = nj * nk
    own = ja * nk + ka
    rows = out_ref.shape[0]
    rank = out_ref.shape[1]
    per_owner = rows // chunk_rows
    chunks = n_owner * per_owner

    def owner_at(turn):
        return lax.rem(own + 1 + turn, n_owner)

    def x_copy(c):
        start = owner_at(c // per_owner) * rows + lax.rem(c, per_owner) * chunk_rows
        slot = lax.rem(c, buffers)
        return pltpu.make_async_copy(
            x_hbm.at[pl.ds(start, chunk_rows)], x_buf.at[slot], x_sem.at[slot]
        )

    def start_x(c, carry):
        x_copy(c).start()
        return carry

    early = min(EARLY, buffers)
    lax.fori_loop(0, early, start_x, 0)

    def third_peer(d):
        at = lax.rem(ia * nj + ja + d, na * nj)
        return at // nj, lax.rem(at, nj)

    def second_peer(d):
        at = lax.rem(ia * nk + ka + d, na * nk)
        return at // nk, lax.rem(at, nk)

    barrier = pltpu.get_barrier_semaphore()

    def greet(device):
        pl.semaphore_signal(barrier, inc=1, device_id=device, device_id_type=MESH)

    def greet_third(d, carry):
        pa, pj = third_peer(d)
        greet((pa, pj, ka))
        return carry

    lax.fori_loop(1, na * nj, greet_third, 0)
    for dk in range(1, nk):
        pk = lax.rem(ka + dk, nk)
        for da in range(na):
            greet((lax.rem(ia + da, na), ja, pk))
        for dj in range(1, nj):
            greet((ia, lax.rem(ja + dj, nj), pk))
    pl.semaphore_wait(barrier, na * nj - 1 + (nk - 1) * (na + nj - 1))

    third_at = ia * nj + ja
    second_at = ia * nk + ka

    def third_copy(d):
        pa, pj = third_peer(d)
        return pltpu.make_async_remote_copy(
            src_ref=third_ref, dst_ref=third_all.at[third_at],
            send_sem=third_send.at[d], recv_sem=third_recv.at[third_at],
            device_id=(pa, pj, ka), device_id_type=MESH,
        )

    def second_copy(d):
        pa, pk = second_peer(d)
        return pltpu.make_async_remote_copy(
            src_ref=second_ref, dst_ref=second_all.at[second_at],
            send_sem=second_send.at[d], recv_sem=second_recv.at[second_at],
            device_id=(pa, ja, pk), device_id_type=MESH,
        )

    def start_third(d, carry):
        third_copy(d).start()
        return carry

    def start_second(d, carry):
        second_copy(d).start()
        return carry

    lax.fori_loop(1, na * nj, start_third, 0)
    lax.fori_loop(1, na * nk, start_second, 0)
    lax.fori_loop(early, buffers, start_x, 0)
    third_all[third_at] = third_ref[...]
    second_all[second_at] = second_ref[...]

    def recv_third(d, carry):
        pa, pj = third_peer(d)
        at = pa * nj + pj
        pltpu.make_async_remote_copy(
            src_ref=third_ref, dst_ref=third_all.at[at],
            send_sem=third_send.at[d], recv_sem=third_recv.at[at],
            device_id=(pa, pj, ka), device_id_type=MESH,
        ).wait_recv()
        return carry

    def recv_second(d, carry):
        pa, pk = second_peer(d)
        at = pa * nk + pk
        pltpu.make_async_remote_copy(
            src_ref=second_ref, dst_ref=second_all.at[at],
            send_sem=second_send.at[d], recv_sem=second_recv.at[at],
            device_id=(pa, ja, pk), device_id_type=MESH,
        ).wait_recv()
        return carry

    lax.fori_loop(1, na * nj, recv_third, 0)
    lax.fori_loop(1, na * nk, recv_second, 0)

    depth = third_ref.shape[0]
    for s in range(na * nj):
        third_flat[s * depth:(s + 1) * depth, :] = third_all[s]
    width = second_ref.shape[0]
    for s in range(na * nk):
        second_flat[s * width:(s + 1) * width, :] = second_all[s]

    third = third_flat[...]
    second = second_flat[...]
    high, low = split(third)
    both = jnp.concatenate([high, low], axis=1)
    weights[...] = jnp.concatenate([both, both], axis=0)
    scale[...] = jnp.concatenate([second, second], axis=1)

    over_rows = (((0,), (0,)), ((), ()))
    gram3[ka] = lax.dot_general(
        third, third, over_rows, precision=HIGHEST, preferred_element_type=jnp.float32
    )
    gram2[ja] = lax.dot_general(
        second, second, over_rows, precision=HIGHEST, preferred_element_type=jnp.float32
    )

    def gram3_copy(d, at):
        return pltpu.make_async_remote_copy(
            src_ref=gram3.at[at], dst_ref=gram3.at[at],
            send_sem=gram3_send.at[d], recv_sem=gram3_recv.at[at],
            device_id=(ia, ja, lax.rem(ka + d, nk)), device_id_type=MESH,
        )

    def gram2_copy(d, at):
        return pltpu.make_async_remote_copy(
            src_ref=gram2.at[at], dst_ref=gram2.at[at],
            send_sem=gram2_send.at[d], recv_sem=gram2_recv.at[at],
            device_id=(ia, lax.rem(ja + d, nj), ka), device_id_type=MESH,
        )

    for d in range(1, nk):
        gram3_copy(d, ka).start()
    for d in range(1, nj):
        gram2_copy(d, ja).start()

    columns = x_hbm.shape[1]
    inner = x_hbm.shape[2]
    together = min(TOGETHER, chunk_rows)

    def chunk(c, carry):
        slot = lax.rem(c, buffers)
        x_copy(c).wait()
        base = lax.rem(c, per_owner) * chunk_rows

        def few(g, carry):
            i = g * together
            x = x_buf[slot, pl.ds(i, together)].reshape(together * columns, inner)
            high, low = split(x)
            y = jnp.dot(
                jnp.concatenate([high, low], axis=1), weights[...],
                preferred_element_type=jnp.float32,
            )
            y = y.reshape(together, columns // 8, 8, 2 * rank)
            y = y * scale[...].reshape(columns // 8, 8, 2 * rank)[None]
            part[pl.ds(base + i, together)] = jnp.sum(y, axis=1)
            return carry

        lax.fori_loop(0, chunk_rows // together, few, 0)

        @pl.when(c + buffers < chunks)
        def _():
            x_copy(c + buffers).start()

        return carry

    def term():
        both = jnp.sum(part[...], axis=1)
        return both[:, :rank] + both[:, rank:]

    def term_copy(turn):
        owner = owner_at(turn)
        return pltpu.make_async_remote_copy(
            src_ref=terms_out.at[turn], dst_ref=terms_in.at[own],
            send_sem=term_send.at[turn], recv_sem=term_recv.at[own],
            device_id=(ia, owner // nk, lax.rem(owner, nk)), device_id_type=MESH,
        )

    def for_other(turn, carry):
        lax.fori_loop(turn * per_owner, (turn + 1) * per_owner, chunk, 0)
        terms_out[turn] = term()
        term_copy(turn).start()
        return carry

    lax.fori_loop(0, n_owner - 1, for_other, 0)
    lax.fori_loop((n_owner - 1) * per_owner, n_owner * per_owner, chunk, 0)
    terms_in[own] = term()

    for d in range(1, nk):
        gram3_copy(d, lax.rem(ka + d, nk)).wait_recv()
    for d in range(1, nj):
        gram2_copy(d, lax.rem(ja + d, nj)).wait_recv()
    mixed = jnp.sum(gram2[...], axis=0) * jnp.sum(gram3[...], axis=0)
    gradient = jnp.dot(
        first_ref[...], mixed, precision=HIGHEST, preferred_element_type=jnp.float32
    )

    def recv_term(turn, carry):
        owner = owner_at(turn)
        pltpu.make_async_remote_copy(
            src_ref=terms_out.at[turn], dst_ref=terms_in.at[owner],
            send_sem=term_send.at[turn], recv_sem=term_recv.at[owner],
            device_id=(ia, owner // nk, lax.rem(owner, nk)), device_id_type=MESH,
        ).wait_recv()
        return carry

    lax.fori_loop(0, n_owner - 1, recv_term, 0)
    out_ref[...] = gradient - jnp.sum(terms_in[...], axis=0)

    def sent_third(d, carry):
        third_copy(d).wait_send()
        return carry

    def sent_second(d, carry):
        second_copy(d).wait_send()
        return carry

    def sent_term(turn, carry):
        term_copy(turn).wait_send()
        return carry

    lax.fori_loop(1, na * nj, sent_third, 0)
    lax.fori_loop(1, na * nk, sent_second, 0)
    for d in range(1, nk):
        gram3_copy(d, ka).wait_send()
    for d in range(1, nj):
        gram2_copy(d, ja).wait_send()
    lax.fori_loop(0, n_owner - 1, sent_term, 0)


def on_device(na, nj, nk, tensor, first, second, third):
    rows, rank = first.shape
    _, columns, inner = tensor.shape
    chunk_rows = min(CHUNK_ROWS, rows)
    buffers = min(BUFFERS, nj * nk * (rows // chunk_rows))
    dma = pltpu.SemaphoreType.DMA
    f32 = jnp.float32
    vmem = pl.BlockSpec(memory_space=pltpu.VMEM)
    return pl.pallas_call(
        functools.partial(kernel, na, nj, nk, chunk_rows, buffers),
        out_shape=jax.ShapeDtypeStruct((rows, rank), f32),
        in_specs=[pl.BlockSpec(memory_space=pl.ANY), vmem, vmem, vmem],
        out_specs=vmem,
        scratch_shapes=[
            pltpu.VMEM((buffers, chunk_rows, columns, inner), f32),
            dma((buffers,)),
            pltpu.VMEM((na * nj,) + third.shape, f32),
            dma((na * nj,)),
            dma((na * nj,)),
            pltpu.VMEM((na * nk,) + second.shape, f32),
            dma((na * nk,)),
            dma((na * nk,)),
            pltpu.VMEM((inner, rank), f32),
            pltpu.VMEM((columns, rank), f32),
            pltpu.VMEM((2 * inner, 2 * rank), jnp.bfloat16),
            pltpu.VMEM((columns, 2 * rank), f32),
            pltpu.VMEM((nk, rank, rank), f32),
            dma((nk,)),
            dma((nk,)),
            pltpu.VMEM((nj, rank, rank), f32),
            dma((nj,)),
            dma((nj,)),
            pltpu.VMEM((rows, 8, 2 * rank), f32),
            pltpu.VMEM((nj * nk, rows, rank), f32),
            pltpu.VMEM((nj * nk, rows, rank), f32),
            dma((nj * nk,)),
            dma((nj * nk,)),
        ],
        compiler_params=pltpu.CompilerParams(
            collective_id=0, has_side_effects=True, vmem_limit_bytes=56 * 2**20
        ),
        name="cp_gradient",
    )(tensor, first, second, third)


def solution(mesh):
    sizes = (mesh.shape["ia"], mesh.shape["ja"], mesh.shape["ka"])
    return jax.shard_map(
        functools.partial(on_device, *sizes),
        mesh=mesh,
        in_specs=(
            P("ia", "ja", "ka"),
            P(("ia", "ja", "ka"), None),
            P(("ja", "ia", "ka"), None),
            P(("ka", "ia", "ja"), None),
        ),
        out_specs=P(("ia", "ja", "ka"), None),
        check_vma=False,
    )
```

```python
import functools

import jax
import jax.numpy as jnp
from jax import lax
from jax.experimental import pallas as pl
from jax.experimental.pallas import tpu as pltpu
from jax.sharding import PartitionSpec as P

MESH = pl.DeviceIdType.MESH
HIGHEST = lax.Precision.HIGHEST
PER_DOT = 4
CHUNK_ROWS = 16
BUFFERS = 10
EARLY = 2


def split(x):
    high = x.astype(jnp.bfloat16)
    low = (x - high.astype(jnp.float32)).astype(jnp.bfloat16)
    return high, low


def kernel(
    na, nj, nk, chunk_rows, buffers,
    x_hbm, first_ref, second_ref, third_ref, out_ref,
    x_buf, x_sem,
    third_all, third_send, third_recv,
    second_all, second_send, second_recv,
    third_flat, second_flat, weights, scale,
    gram3, gram3_send, gram3_recv,
    gram2, gram2_send, gram2_recv,
    part, terms_out, terms_in, term_send, term_recv,
):
    ia, ja, ka = lax.axis_index("ia"), lax.axis_index("ja"), lax.axis_index("ka")
    n_owner = nj * nk
    own = ja * nk + ka
    rows = out_ref.shape[0]
    rank = out_ref.shape[1]
    per_owner = rows // chunk_rows
    chunks = n_owner * per_owner

    def owner_at(turn):
        return lax.rem(own + 1 + turn, n_owner)

    def x_copy(c):
        start = owner_at(c // per_owner) * rows + lax.rem(c, per_owner) * chunk_rows
        slot = lax.rem(c, buffers)
        return pltpu.make_async_copy(
            x_hbm.at[pl.ds(start, chunk_rows)], x_buf.at[slot], x_sem.at[slot]
        )

    def start_x(c, carry):
        x_copy(c).start()
        return carry

    def third_peer(d):
        at = lax.rem(ia * nj + ja + d, na * nj)
        return at // nj, lax.rem(at, nj)

    def second_peer(d):
        at = lax.rem(ia * nk + ka + d, na * nk)
        return at // nk, lax.rem(at, nk)

    barrier = pltpu.get_barrier_semaphore()

    def greet(device):
        pl.semaphore_signal(barrier, inc=1, device_id=device, device_id_type=MESH)

    def greet_third(d, carry):
        pa, pj = third_peer(d)
        greet((pa, pj, ka))
        return carry

    lax.fori_loop(1, na * nj, greet_third, 0)
    for dk in range(1, nk):
        pk = lax.rem(ka + dk, nk)
        for da in range(na):
            greet((lax.rem(ia + da, na), ja, pk))
        for dj in range(1, nj):
            greet((ia, lax.rem(ja + dj, nj), pk))
    early = min(EARLY, buffers)
    lax.fori_loop(0, early, start_x, 0)
    pl.semaphore_wait(barrier, na * nj - 1 + (nk - 1) * (na + nj - 1))

    third_at = ia * nj + ja
    second_at = ia * nk + ka

    def third_copy(d):
        pa, pj = third_peer(d)
        return pltpu.make_async_remote_copy(
            src_ref=third_ref, dst_ref=third_all.at[third_at],
            send_sem=third_send.at[d], recv_sem=third_recv.at[third_at],
            device_id=(pa, pj, ka), device_id_type=MESH,
        )

    def second_copy(d):
        pa, pk = second_peer(d)
        return pltpu.make_async_remote_copy(
            src_ref=second_ref, dst_ref=second_all.at[second_at],
            send_sem=second_send.at[d], recv_sem=second_recv.at[second_at],
            device_id=(pa, ja, pk), device_id_type=MESH,
        )

    def start_third(d, carry):
        third_copy(d).start()
        return carry

    def start_second(d, carry):
        second_copy(d).start()
        return carry

    lax.fori_loop(1, na * nj, start_third, 0)
    lax.fori_loop(1, na * nk, start_second, 0)
    lax.fori_loop(early, buffers, start_x, 0)
    third_all[third_at] = third_ref[...]
    second_all[second_at] = second_ref[...]

    def recv_third(d, carry):
        pa, pj = third_peer(d)
        at = pa * nj + pj
        pltpu.make_async_remote_copy(
            src_ref=third_ref, dst_ref=third_all.at[at],
            send_sem=third_send.at[d], recv_sem=third_recv.at[at],
            device_id=(pa, pj, ka), device_id_type=MESH,
        ).wait_recv()
        return carry

    def recv_second(d, carry):
        pa, pk = second_peer(d)
        at = pa * nk + pk
        pltpu.make_async_remote_copy(
            src_ref=second_ref, dst_ref=second_all.at[at],
            send_sem=second_send.at[d], recv_sem=second_recv.at[at],
            device_id=(pa, ja, pk), device_id_type=MESH,
        ).wait_recv()
        return carry

    lax.fori_loop(1, na * nj, recv_third, 0)
    lax.fori_loop(1, na * nk, recv_second, 0)

    depth = third_ref.shape[0]
    for s in range(na * nj):
        third_flat[s * depth:(s + 1) * depth, :] = third_all[s]
    width = second_ref.shape[0]
    for s in range(na * nk):
        second_flat[s * width:(s + 1) * width, :] = second_all[s]

    third = third_flat[...]
    second = second_flat[...]
    both3 = jnp.concatenate(split(third), axis=1)
    both2 = jnp.concatenate(split(second), axis=1)
    weights[...] = jnp.concatenate([both3, both3], axis=0)
    scale[...] = jnp.concatenate([second, second], axis=1)

    def gram_of(both):
        pairs = lax.dot_general(
            both, both, (((0,), (0,)), ((), ())), preferred_element_type=jnp.float32
        )
        halves = pairs[:rank] + pairs[rank:]
        return halves[:, :rank] + halves[:, rank:]

    gram3[ka] = gram_of(both3)
    gram2[ja] = gram_of(both2)

    def gram3_copy(d, at):
        return pltpu.make_async_remote_copy(
            src_ref=gram3.at[at], dst_ref=gram3.at[at],
            send_sem=gram3_send.at[d], recv_sem=gram3_recv.at[at],
            device_id=(ia, ja, lax.rem(ka + d, nk)), device_id_type=MESH,
        )

    def gram2_copy(d, at):
        return pltpu.make_async_remote_copy(
            src_ref=gram2.at[at], dst_ref=gram2.at[at],
            send_sem=gram2_send.at[d], recv_sem=gram2_recv.at[at],
            device_id=(ia, lax.rem(ja + d, nj), ka), device_id_type=MESH,
        )

    for d in range(1, nk):
        gram3_copy(d, ka).start()
    for d in range(1, nj):
        gram2_copy(d, ja).start()

    columns = x_hbm.shape[1]
    inner = x_hbm.shape[2]
    per = min(PER_DOT, chunk_rows)

    def chunk(c, carry):
        slot = lax.rem(c, buffers)
        x_copy(c).wait()
        sums = []
        for i in range(0, chunk_rows, per):
            x = x_buf[slot, i:i + per].reshape(per * columns, inner)
            y = jnp.dot(
                jnp.concatenate(split(x), axis=1), weights[...],
                preferred_element_type=jnp.float32,
            )
            y = y.reshape(per, columns, 2 * rank) * scale[...][None]
            sums.append(jnp.sum(y, axis=1))
        base = pl.multiple_of(lax.rem(c, per_owner) * chunk_rows, chunk_rows)
        part[pl.ds(base, chunk_rows)] = jnp.concatenate(sums, axis=0)

        @pl.when(c + buffers < chunks)
        def _():
            x_copy(c + buffers).start()

        return carry

    def term_copy(turn):
        owner = owner_at(turn)
        return pltpu.make_async_remote_copy(
            src_ref=terms_out.at[turn], dst_ref=terms_in.at[own],
            send_sem=term_send.at[turn], recv_sem=term_recv.at[own],
            device_id=(ia, owner // nk, lax.rem(owner, nk)), device_id_type=MESH,
        )

    def for_owner(turn, carry):
        lax.fori_loop(turn * per_owner, (turn + 1) * per_owner, chunk, 0)
        term = part[:, :rank] + part[:, rank:]

        @pl.when(turn < n_owner - 1)
        def _():
            terms_out[turn] = term
            term_copy(turn).start()

        @pl.when(turn == n_owner - 1)
        def _():
            terms_in[own] = term

        return carry

    lax.fori_loop(0, n_owner, for_owner, 0)

    for d in range(1, nk):
        gram3_copy(d, lax.rem(ka + d, nk)).wait_recv()
    for d in range(1, nj):
        gram2_copy(d, lax.rem(ja + d, nj)).wait_recv()
    mixed = jnp.sum(gram2[...], axis=0) * jnp.sum(gram3[...], axis=0)
    gradient = jnp.dot(
        first_ref[...], mixed, precision=HIGHEST, preferred_element_type=jnp.float32
    )

    def recv_term(turn, carry):
        owner = owner_at(turn)
        pltpu.make_async_remote_copy(
            src_ref=terms_out.at[turn], dst_ref=terms_in.at[owner],
            send_sem=term_send.at[turn], recv_sem=term_recv.at[owner],
            device_id=(ia, owner // nk, lax.rem(owner, nk)), device_id_type=MESH,
        ).wait_recv()
        return carry

    lax.fori_loop(0, n_owner - 1, recv_term, 0)
    out_ref[...] = gradient - jnp.sum(terms_in[...], axis=0)

    def sent_third(d, carry):
        third_copy(d).wait_send()
        return carry

    def sent_second(d, carry):
        second_copy(d).wait_send()
        return carry

    def sent_term(turn, carry):
        term_copy(turn).wait_send()
        return carry

    lax.fori_loop(1, na * nj, sent_third, 0)
    lax.fori_loop(1, na * nk, sent_second, 0)
    for d in range(1, nk):
        gram3_copy(d, ka).wait_send()
    for d in range(1, nj):
        gram2_copy(d, ja).wait_send()
    lax.fori_loop(0, n_owner - 1, sent_term, 0)


def on_device(na, nj, nk, tensor, first, second, third):
    rows, rank = first.shape
    _, columns, inner = tensor.shape
    chunk_rows = min(CHUNK_ROWS, rows)
    buffers = min(BUFFERS, nj * nk * (rows // chunk_rows))
    dma = pltpu.SemaphoreType.DMA
    f32 = jnp.float32
    vmem = pl.BlockSpec(memory_space=pltpu.VMEM)
    return pl.pallas_call(
        functools.partial(kernel, na, nj, nk, chunk_rows, buffers),
        out_shape=jax.ShapeDtypeStruct((rows, rank), f32),
        in_specs=[pl.BlockSpec(memory_space=pl.ANY), vmem, vmem, vmem],
        out_specs=vmem,
        scratch_shapes=[
            pltpu.VMEM((buffers, chunk_rows, columns, inner), f32),
            dma((buffers,)),
            pltpu.VMEM((na * nj,) + third.shape, f32),
            dma((na * nj,)),
            dma((na * nj,)),
            pltpu.VMEM((na * nk,) + second.shape, f32),
            dma((na * nk,)),
            dma((na * nk,)),
            pltpu.VMEM((inner, rank), f32),
            pltpu.VMEM((columns, rank), f32),
            pltpu.VMEM((2 * inner, 2 * rank), jnp.bfloat16),
            pltpu.VMEM((columns, 2 * rank), f32),
            pltpu.VMEM((nk, rank, rank), f32),
            dma((nk,)),
            dma((nk,)),
            pltpu.VMEM((nj, rank, rank), f32),
            dma((nj,)),
            dma((nj,)),
            pltpu.VMEM((rows, 2 * rank), f32),
            pltpu.VMEM((nj * nk, rows, rank), f32),
            pltpu.VMEM((nj * nk, rows, rank), f32),
            dma((nj * nk,)),
            dma((nj * nk,)),
        ],
        compiler_params=pltpu.CompilerParams(
            collective_id=0, has_side_effects=True, vmem_limit_bytes=56 * 2**20
        ),
        name="cp_gradient",
    )(tensor, first, second, third)


def solution(mesh):
    sizes = (mesh.shape["ia"], mesh.shape["ja"], mesh.shape["ka"])
    return jax.shard_map(
        functools.partial(on_device, *sizes),
        mesh=mesh,
        in_specs=(
            P("ia", "ja", "ka"),
            P(("ia", "ja", "ka"), None),
            P(("ja", "ia", "ka"), None),
            P(("ka", "ia", "ja"), None),
        ),
        out_specs=P(("ia", "ja", "ka"), None),
        check_vma=False,
    )
```

```python
import functools

import jax
import jax.numpy as jnp
from jax import lax
from jax.experimental import pallas as pl
from jax.experimental.pallas import tpu as pltpu
from jax.sharding import PartitionSpec as P

MESH = pl.DeviceIdType.MESH
HIGHEST = lax.Precision.HIGHEST
PER_DOT = 4
CHUNK_ROWS = 16
BUFFERS = 10
EARLY = 2


def split(x):
    high = x.astype(jnp.bfloat16)
    low = (x - high.astype(jnp.float32)).astype(jnp.bfloat16)
    return high, low


def kernel(
    na, nj, nk, chunk_rows, buffers,
    x_hbm, first_ref, second_ref, third_ref, out_ref,
    x_buf, x_sem,
    third_all, third_send, third_recv,
    second_all, second_send, second_recv,
    third_flat, second_flat, weights, scale,
    gram3, gram3_send, gram3_recv,
    gram2, gram2_send, gram2_recv,
    part, terms_out, terms_in, term_send, term_recv,
):
    ia, ja, ka = lax.axis_index("ia"), lax.axis_index("ja"), lax.axis_index("ka")
    n_owner = nj * nk
    own = ja * nk + ka
    rows = out_ref.shape[0]
    rank = out_ref.shape[1]
    per_owner = rows // chunk_rows
    chunks = n_owner * per_owner

    def owner_at(turn):
        return lax.rem(own + 1 + turn, n_owner)

    def x_copy(c):
        start = owner_at(c // per_owner) * rows + lax.rem(c, per_owner) * chunk_rows
        slot = lax.rem(c, buffers)
        return pltpu.make_async_copy(
            x_hbm.at[pl.ds(start, chunk_rows)], x_buf.at[slot], x_sem.at[slot]
        )

    def start_x(c, carry):
        x_copy(c).start()
        return carry

    def third_peer(d):
        at = lax.rem(ia * nj + ja + d, na * nj)
        return at // nj, lax.rem(at, nj)

    def second_peer(d):
        at = lax.rem(ia * nk + ka + d, na * nk)
        return at // nk, lax.rem(at, nk)

    barrier = pltpu.get_barrier_semaphore()

    def greet(device):
        pl.semaphore_signal(barrier, inc=1, device_id=device, device_id_type=MESH)

    def greet_third(d, carry):
        pa, pj = third_peer(d)
        greet((pa, pj, ka))
        return carry

    lax.fori_loop(1, na * nj, greet_third, 0)
    for dk in range(1, nk):
        pk = lax.rem(ka + dk, nk)
        for da in range(na):
            greet((lax.rem(ia + da, na), ja, pk))
        for dj in range(1, nj):
            greet((ia, lax.rem(ja + dj, nj), pk))
    early = min(EARLY, buffers)
    lax.fori_loop(0, early, start_x, 0)
    pl.semaphore_wait(barrier, na * nj - 1 + (nk - 1) * (na + nj - 1))

    third_at = ia * nj + ja
    second_at = ia * nk + ka

    def third_copy(d):
        pa, pj = third_peer(d)
        return pltpu.make_async_remote_copy(
            src_ref=third_ref, dst_ref=third_all.at[third_at],
            send_sem=third_send.at[d], recv_sem=third_recv.at[third_at],
            device_id=(pa, pj, ka), device_id_type=MESH,
        )

    def second_copy(d):
        pa, pk = second_peer(d)
        return pltpu.make_async_remote_copy(
            src_ref=second_ref, dst_ref=second_all.at[second_at],
            send_sem=second_send.at[d], recv_sem=second_recv.at[second_at],
            device_id=(pa, ja, pk), device_id_type=MESH,
        )

    def start_third(d, carry):
        third_copy(d).start()
        return carry

    def start_second(d, carry):
        second_copy(d).start()
        return carry

    lax.fori_loop(1, na * nj, start_third, 0)
    lax.fori_loop(1, na * nk, start_second, 0)
    lax.fori_loop(early, buffers, start_x, 0)
    third_all[third_at] = third_ref[...]
    second_all[second_at] = second_ref[...]

    def recv_third(d, carry):
        pa, pj = third_peer(d)
        at = pa * nj + pj
        pltpu.make_async_remote_copy(
            src_ref=third_ref, dst_ref=third_all.at[at],
            send_sem=third_send.at[d], recv_sem=third_recv.at[at],
            device_id=(pa, pj, ka), device_id_type=MESH,
        ).wait_recv()
        return carry

    def recv_second(d, carry):
        pa, pk = second_peer(d)
        at = pa * nk + pk
        pltpu.make_async_remote_copy(
            src_ref=second_ref, dst_ref=second_all.at[at],
            send_sem=second_send.at[d], recv_sem=second_recv.at[at],
            device_id=(pa, ja, pk), device_id_type=MESH,
        ).wait_recv()
        return carry

    lax.fori_loop(1, na * nj, recv_third, 0)
    lax.fori_loop(1, na * nk, recv_second, 0)

    depth = third_ref.shape[0]
    for s in range(na * nj):
        third_flat[s * depth:(s + 1) * depth, :] = third_all[s]
    width = second_ref.shape[0]
    for s in range(na * nk):
        second_flat[s * width:(s + 1) * width, :] = second_all[s]

    third = third_flat[...]
    second = second_flat[...]
    both3 = jnp.concatenate(split(third), axis=1)
    both2 = jnp.concatenate(split(second), axis=1)
    turned = jnp.concatenate(split(second.T), axis=0)
    weights[...] = jnp.concatenate([turned, turned], axis=1)
    scale[...] = jnp.concatenate([third.T, third.T], axis=0)

    def gram_of(both):
        pairs = lax.dot_general(
            both, both, (((0,), (0,)), ((), ())), preferred_element_type=jnp.float32
        )
        halves = pairs[:rank] + pairs[rank:]
        return halves[:, :rank] + halves[:, rank:]

    gram3[ka] = gram_of(both3)
    gram2[ja] = gram_of(both2)

    def gram3_copy(d, at):
        return pltpu.make_async_remote_copy(
            src_ref=gram3.at[at], dst_ref=gram3.at[at],
            send_sem=gram3_send.at[d], recv_sem=gram3_recv.at[at],
            device_id=(ia, ja, lax.rem(ka + d, nk)), device_id_type=MESH,
        )

    def gram2_copy(d, at):
        return pltpu.make_async_remote_copy(
            src_ref=gram2.at[at], dst_ref=gram2.at[at],
            send_sem=gram2_send.at[d], recv_sem=gram2_recv.at[at],
            device_id=(ia, lax.rem(ja + d, nj), ka), device_id_type=MESH,
        )

    for d in range(1, nk):
        gram3_copy(d, ka).start()
    for d in range(1, nj):
        gram2_copy(d, ja).start()

    columns = x_hbm.shape[1]
    inner = x_hbm.shape[2]
    per = min(PER_DOT, chunk_rows)

    def chunk(c, carry):
        slot = lax.rem(c, buffers)
        x_copy(c).wait()
        base = pl.multiple_of(lax.rem(c, per_owner) * chunk_rows, chunk_rows)
        found = []
        for i in range(chunk_rows):
            high, low = split(x_buf[slot, i])
            z = jnp.dot(
                weights[...], jnp.concatenate([high, low], axis=0),
                preferred_element_type=jnp.float32,
            )
            z = z * scale[...]
            z = z[:rank] + z[rank:]
            found.append(sum(z[:, at:at + 128] for at in range(0, inner, 128)))
        part[pl.ds(base, chunk_rows)] = jnp.stack(found)

        @pl.when(c + buffers < chunks)
        def _():
            x_copy(c + buffers).start()

        return carry

    def term_copy(turn):
        owner = owner_at(turn)
        return pltpu.make_async_remote_copy(
            src_ref=terms_out.at[turn], dst_ref=terms_in.at[own],
            send_sem=term_send.at[turn], recv_sem=term_recv.at[own],
            device_id=(ia, owner // nk, lax.rem(owner, nk)), device_id_type=MESH,
        )

    def for_owner(turn, carry):
        lax.fori_loop(turn * per_owner, (turn + 1) * per_owner, chunk, 0)
        term = jnp.sum(part[...], axis=2)

        @pl.when(turn < n_owner - 1)
        def _():
            terms_out[turn] = term
            term_copy(turn).start()

        @pl.when(turn == n_owner - 1)
        def _():
            terms_in[own] = term

        return carry

    lax.fori_loop(0, n_owner, for_owner, 0)

    for d in range(1, nk):
        gram3_copy(d, lax.rem(ka + d, nk)).wait_recv()
    for d in range(1, nj):
        gram2_copy(d, lax.rem(ja + d, nj)).wait_recv()
    mixed = jnp.sum(gram2[...], axis=0) * jnp.sum(gram3[...], axis=0)
    gradient = jnp.dot(
        first_ref[...], mixed, precision=HIGHEST, preferred_element_type=jnp.float32
    )

    def recv_term(turn, carry):
        owner = owner_at(turn)
        pltpu.make_async_remote_copy(
            src_ref=terms_out.at[turn], dst_ref=terms_in.at[owner],
            send_sem=term_send.at[turn], recv_sem=term_recv.at[owner],
            device_id=(ia, owner // nk, lax.rem(owner, nk)), device_id_type=MESH,
        ).wait_recv()
        return carry

    lax.fori_loop(0, n_owner - 1, recv_term, 0)
    out_ref[...] = gradient - jnp.sum(terms_in[...], axis=0)

    def sent_third(d, carry):
        third_copy(d).wait_send()
        return carry

    def sent_second(d, carry):
        second_copy(d).wait_send()
        return carry

    def sent_term(turn, carry):
        term_copy(turn).wait_send()
        return carry

    lax.fori_loop(1, na * nj, sent_third, 0)
    lax.fori_loop(1, na * nk, sent_second, 0)
    for d in range(1, nk):
        gram3_copy(d, ka).wait_send()
    for d in range(1, nj):
        gram2_copy(d, ja).wait_send()
    lax.fori_loop(0, n_owner - 1, sent_term, 0)


def on_device(na, nj, nk, tensor, first, second, third):
    rows, rank = first.shape
    _, columns, inner = tensor.shape
    chunk_rows = min(CHUNK_ROWS, rows)
    buffers = min(BUFFERS, nj * nk * (rows // chunk_rows))
    dma = pltpu.SemaphoreType.DMA
    f32 = jnp.float32
    vmem = pl.BlockSpec(memory_space=pltpu.VMEM)
    return pl.pallas_call(
        functools.partial(kernel, na, nj, nk, chunk_rows, buffers),
        out_shape=jax.ShapeDtypeStruct((rows, rank), f32),
        in_specs=[pl.BlockSpec(memory_space=pl.ANY), vmem, vmem, vmem],
        out_specs=vmem,
        scratch_shapes=[
            pltpu.VMEM((buffers, chunk_rows, columns, inner), f32),
            dma((buffers,)),
            pltpu.VMEM((na * nj,) + third.shape, f32),
            dma((na * nj,)),
            dma((na * nj,)),
            pltpu.VMEM((na * nk,) + second.shape, f32),
            dma((na * nk,)),
            dma((na * nk,)),
            pltpu.VMEM((inner, rank), f32),
            pltpu.VMEM((columns, rank), f32),
            pltpu.VMEM((2 * rank, 2 * columns), jnp.bfloat16),
            pltpu.VMEM((2 * rank, inner), f32),
            pltpu.VMEM((nk, rank, rank), f32),
            dma((nk,)),
            dma((nk,)),
            pltpu.VMEM((nj, rank, rank), f32),
            dma((nj,)),
            dma((nj,)),
            pltpu.VMEM((rows, rank, 128), f32),
            pltpu.VMEM((nj * nk, rows, rank), f32),
            pltpu.VMEM((nj * nk, rows, rank), f32),
            dma((nj * nk,)),
            dma((nj * nk,)),
        ],
        compiler_params=pltpu.CompilerParams(
            collective_id=0, has_side_effects=True, vmem_limit_bytes=56 * 2**20
        ),
        name="cp_gradient",
    )(tensor, first, second, third)


def solution(mesh):
    sizes = (mesh.shape["ia"], mesh.shape["ja"], mesh.shape["ka"])
    return jax.shard_map(
        functools.partial(on_device, *sizes),
        mesh=mesh,
        in_specs=(
            P("ia", "ja", "ka"),
            P(("ia", "ja", "ka"), None),
            P(("ja", "ia", "ka"), None),
            P(("ka", "ia", "ja"), None),
        ),
        out_specs=P(("ia", "ja", "ka"), None),
        check_vma=False,
    )
```

```python
import functools

import jax
import jax.numpy as jnp
from jax import lax
from jax.experimental import pallas as pl
from jax.experimental.pallas import tpu as pltpu
from jax.sharding import PartitionSpec as P

MESH = pl.DeviceIdType.MESH
HIGHEST = lax.Precision.HIGHEST
BUFFERS = 5
EARLY = 1


def split(x):
    high = x.astype(jnp.bfloat16)
    low = (x - high.astype(jnp.float32)).astype(jnp.bfloat16)
    return high, low


def kernel(
    na, nj, nk, buffers,
    x_hbm, first_ref, second_ref, third_ref, out_ref,
    x_buf, x_sem,
    third_all, third_send, third_recv,
    second_all, second_send, second_recv,
    third_flat, second_flat, weights, scale,
    gram3, gram3_send, gram3_recv,
    gram2, gram2_send, gram2_recv,
    terms_out, terms_in, term_send, term_recv,
):
    ia, ja, ka = lax.axis_index("ia"), lax.axis_index("ja"), lax.axis_index("ka")
    n_owner = nj * nk
    own = ja * nk + ka
    rows = out_ref.shape[0]
    rank = out_ref.shape[1]

    def owner_at(turn):
        return lax.rem(own + 1 + turn, n_owner)

    def x_copy(turn):
        slot = lax.rem(turn, buffers)
        return pltpu.make_async_copy(
            x_hbm.at[pl.ds(owner_at(turn) * rows, rows)], x_buf.at[slot], x_sem.at[slot]
        )

    def start_x(c, carry):
        x_copy(c).start()
        return carry

    def third_peer(d):
        at = lax.rem(ia * nj + ja + d, na * nj)
        return at // nj, lax.rem(at, nj)

    def second_peer(d):
        at = lax.rem(ia * nk + ka + d, na * nk)
        return at // nk, lax.rem(at, nk)

    barrier = pltpu.get_barrier_semaphore()

    def greet(device):
        pl.semaphore_signal(barrier, inc=1, device_id=device, device_id_type=MESH)

    def greet_third(d, carry):
        pa, pj = third_peer(d)
        greet((pa, pj, ka))
        return carry

    lax.fori_loop(1, na * nj, greet_third, 0)
    for dk in range(1, nk):
        pk = lax.rem(ka + dk, nk)
        for da in range(na):
            greet((lax.rem(ia + da, na), ja, pk))
        for dj in range(1, nj):
            greet((ia, lax.rem(ja + dj, nj), pk))
    early = min(EARLY, buffers)
    lax.fori_loop(0, early, start_x, 0)
    pl.semaphore_wait(barrier, na * nj - 1 + (nk - 1) * (na + nj - 1))

    third_at = ia * nj + ja
    second_at = ia * nk + ka

    def third_copy(d):
        pa, pj = third_peer(d)
        return pltpu.make_async_remote_copy(
            src_ref=third_ref, dst_ref=third_all.at[third_at],
            send_sem=third_send.at[d], recv_sem=third_recv.at[third_at],
            device_id=(pa, pj, ka), device_id_type=MESH,
        )

    def second_copy(d):
        pa, pk = second_peer(d)
        return pltpu.make_async_remote_copy(
            src_ref=second_ref, dst_ref=second_all.at[second_at],
            send_sem=second_send.at[d], recv_sem=second_recv.at[second_at],
            device_id=(pa, ja, pk), device_id_type=MESH,
        )

    def start_third(d, carry):
        third_copy(d).start()
        return carry

    def start_second(d, carry):
        second_copy(d).start()
        return carry

    lax.fori_loop(1, na * nk, start_second, 0)
    lax.fori_loop(1, na * nj, start_third, 0)
    lax.fori_loop(early, buffers, start_x, 0)
    third_all[third_at] = third_ref[...]
    second_all[second_at] = second_ref[...]

    def recv_third(d, carry):
        pa, pj = third_peer(d)
        at = pa * nj + pj
        pltpu.make_async_remote_copy(
            src_ref=third_ref, dst_ref=third_all.at[at],
            send_sem=third_send.at[d], recv_sem=third_recv.at[at],
            device_id=(pa, pj, ka), device_id_type=MESH,
        ).wait_recv()
        return carry

    def recv_second(d, carry):
        pa, pk = second_peer(d)
        at = pa * nk + pk
        pltpu.make_async_remote_copy(
            src_ref=second_ref, dst_ref=second_all.at[at],
            send_sem=second_send.at[d], recv_sem=second_recv.at[at],
            device_id=(pa, ja, pk), device_id_type=MESH,
        ).wait_recv()
        return carry

    def gram3_copy(d, at):
        return pltpu.make_async_remote_copy(
            src_ref=gram3.at[at], dst_ref=gram3.at[at],
            send_sem=gram3_send.at[d], recv_sem=gram3_recv.at[at],
            device_id=(ia, ja, lax.rem(ka + d, nk)), device_id_type=MESH,
        )

    def gram2_copy(d, at):
        return pltpu.make_async_remote_copy(
            src_ref=gram2.at[at], dst_ref=gram2.at[at],
            send_sem=gram2_send.at[d], recv_sem=gram2_recv.at[at],
            device_id=(ia, lax.rem(ja + d, nj), ka), device_id_type=MESH,
        )

    def gram_of(turned):
        pairs = lax.dot_general(
            turned, turned, (((1,), (1,)), ((), ())), preferred_element_type=jnp.float32
        )
        halves = pairs[:rank] + pairs[rank:]
        return halves[:, :rank] + halves[:, rank:]

    lax.fori_loop(1, na * nk, recv_second, 0)
    width = second_ref.shape[0]
    for s in range(na * nk):
        second_flat[s * width:(s + 1) * width, :] = second_all[s]
    turned2 = jnp.concatenate(split(second_flat[...].T), axis=0)
    weights[...] = jnp.concatenate([turned2, turned2], axis=1)
    gram2[ja] = gram_of(turned2)
    for d in range(1, nj):
        gram2_copy(d, ja).start()

    lax.fori_loop(1, na * nj, recv_third, 0)
    depth = third_ref.shape[0]
    for s in range(na * nj):
        third_flat[s * depth:(s + 1) * depth, :] = third_all[s]
    third = third_flat[...].T
    scale[...] = jnp.concatenate([third, third], axis=0)
    gram3[ka] = gram_of(jnp.concatenate(split(third), axis=0))
    for d in range(1, nk):
        gram3_copy(d, ka).start()

    inner = x_hbm.shape[2]

    def term_copy(turn):
        owner = owner_at(turn)
        return pltpu.make_async_remote_copy(
            src_ref=terms_out.at[turn], dst_ref=terms_in.at[own],
            send_sem=term_send.at[turn], recv_sem=term_recv.at[own],
            device_id=(ia, owner // nk, lax.rem(owner, nk)), device_id_type=MESH,
        )

    def for_owner(turn, carry):
        slot = lax.rem(turn, buffers)
        x_copy(turn).wait()
        found = []
        for i in range(rows):
            z = jnp.dot(
                weights[...], jnp.concatenate(split(x_buf[slot, i]), axis=0),
                preferred_element_type=jnp.float32,
            )
            z = z * scale[...]
            z = z[:rank] + z[rank:]
            found.append(sum(z[:, at:at + 128] for at in range(0, inner, 128)))
        term = jnp.sum(jnp.stack(found), axis=2)

        @pl.when(turn + buffers < n_owner)
        def _():
            x_copy(turn + buffers).start()

        @pl.when(turn < n_owner - 1)
        def _():
            terms_out[turn] = term
            term_copy(turn).start()

        @pl.when(turn == n_owner - 1)
        def _():
            terms_in[own] = term

        return carry

    lax.fori_loop(0, n_owner, for_owner, 0)

    for d in range(1, nk):
        gram3_copy(d, lax.rem(ka + d, nk)).wait_recv()
    for d in range(1, nj):
        gram2_copy(d, lax.rem(ja + d, nj)).wait_recv()
    mixed = jnp.sum(gram2[...], axis=0) * jnp.sum(gram3[...], axis=0)
    gradient = jnp.dot(
        first_ref[...], mixed, precision=HIGHEST, preferred_element_type=jnp.float32
    )

    def recv_term(turn, carry):
        owner = owner_at(turn)
        pltpu.make_async_remote_copy(
            src_ref=terms_out.at[turn], dst_ref=terms_in.at[owner],
            send_sem=term_send.at[turn], recv_sem=term_recv.at[owner],
            device_id=(ia, owner // nk, lax.rem(owner, nk)), device_id_type=MESH,
        ).wait_recv()
        return carry

    lax.fori_loop(0, n_owner - 1, recv_term, 0)
    out_ref[...] = jnp.sum(terms_in[...], axis=0) - gradient

    def sent_third(d, carry):
        third_copy(d).wait_send()
        return carry

    def sent_second(d, carry):
        second_copy(d).wait_send()
        return carry

    def sent_term(turn, carry):
        term_copy(turn).wait_send()
        return carry

    lax.fori_loop(1, na * nj, sent_third, 0)
    lax.fori_loop(1, na * nk, sent_second, 0)
    for d in range(1, nk):
        gram3_copy(d, ka).wait_send()
    for d in range(1, nj):
        gram2_copy(d, ja).wait_send()
    lax.fori_loop(0, n_owner - 1, sent_term, 0)


def on_device(na, nj, nk, tensor, first, second, third):
    rows, rank = first.shape
    _, columns, inner = tensor.shape
    buffers = min(BUFFERS, nj * nk)
    dma = pltpu.SemaphoreType.DMA
    f32 = jnp.float32
    vmem = pl.BlockSpec(memory_space=pltpu.VMEM)
    return -pl.pallas_call(
        functools.partial(kernel, na, nj, nk, buffers),
        out_shape=jax.ShapeDtypeStruct((rows, rank), f32),
        in_specs=[pl.BlockSpec(memory_space=pl.ANY), vmem, vmem, vmem],
        out_specs=vmem,
        scratch_shapes=[
            pltpu.VMEM((buffers, rows, columns, inner), f32),
            dma((buffers,)),
            pltpu.VMEM((na * nj,) + third.shape, f32),
            dma((na * nj,)),
            dma((na * nj,)),
            pltpu.VMEM((na * nk,) + second.shape, f32),
            dma((na * nk,)),
            dma((na * nk,)),
            pltpu.VMEM((inner, rank), f32),
            pltpu.VMEM((columns, rank), f32),
            pltpu.VMEM((2 * rank, 2 * columns), jnp.bfloat16),
            pltpu.VMEM((2 * rank, inner), f32),
            pltpu.VMEM((nk, rank, rank), f32),
            dma((nk,)),
            dma((nk,)),
            pltpu.VMEM((nj, rank, rank), f32),
            dma((nj,)),
            dma((nj,)),
            pltpu.VMEM((nj * nk, rows, rank), f32),
            pltpu.VMEM((nj * nk, rows, rank), f32),
            dma((nj * nk,)),
            dma((nj * nk,)),
        ],
        compiler_params=pltpu.CompilerParams(
            collective_id=0, has_side_effects=True, vmem_limit_bytes=48 * 2**20
        ),
        name="cp_gradient",
    )(tensor, first, second, third)


def solution(mesh):
    sizes = (mesh.shape["ia"], mesh.shape["ja"], mesh.shape["ka"])
    return jax.shard_map(
        functools.partial(on_device, *sizes),
        mesh=mesh,
        in_specs=(
            P("ia", "ja", "ka"),
            P(("ia", "ja", "ka"), None),
            P(("ja", "ia", "ka"), None),
            P(("ka", "ia", "ja"), None),
        ),
        out_specs=P(("ia", "ja", "ka"), None),
        check_vma=False,
    )
```

```python
import functools

import jax
import jax.numpy as jnp
from jax import lax
from jax.experimental import pallas as pl
from jax.experimental.pallas import tpu as pltpu
from jax.sharding import PartitionSpec as P

MESH = pl.DeviceIdType.MESH
HIGHEST = lax.Precision.HIGHEST
BUFFERS = 5
EARLY = 1


def split(x):
    high = x.astype(jnp.bfloat16)
    low = (x - high.astype(jnp.float32)).astype(jnp.bfloat16)
    return high, low


def kernel(
    na, nj, nk, buffers,
    x_hbm, first_hbm, second_hbm, third_hbm, out_ref,
    first_ref, near_sem,
    x_buf, x_sem,
    third_all, third_send, third_recv,
    second_all, second_send, second_recv,
    third_flat, second_flat, weights, scale,
    gram3, gram3_send, gram3_recv,
    gram2, gram2_send, gram2_recv,
    terms_out, terms_in, term_send, term_recv,
):
    ia, ja, ka = lax.axis_index("ia"), lax.axis_index("ja"), lax.axis_index("ka")
    n_owner = nj * nk
    own = ja * nk + ka
    rows = out_ref.shape[0]
    rank = out_ref.shape[1]

    def owner_at(turn):
        return lax.rem(own + 1 + turn, n_owner)

    def x_copy(turn):
        slot = lax.rem(turn, buffers)
        return pltpu.make_async_copy(
            x_hbm.at[pl.ds(owner_at(turn) * rows, rows)], x_buf.at[slot], x_sem.at[slot]
        )

    def start_x(c, carry):
        x_copy(c).start()
        return carry

    third_at = ia * nj + ja
    second_at = ia * nk + ka
    third_ref, second_ref = third_all.at[third_at], second_all.at[second_at]
    near = [
        pltpu.make_async_copy(source, target, near_sem.at[k])
        for k, (source, target) in enumerate(
            [(second_hbm, second_ref), (third_hbm, third_ref), (first_hbm, first_ref)]
        )
    ]
    for copy in near:
        copy.start()

    def third_peer(d):
        at = lax.rem(ia * nj + ja + d, na * nj)
        return at // nj, lax.rem(at, nj)

    def second_peer(d):
        at = lax.rem(ia * nk + ka + d, na * nk)
        return at // nk, lax.rem(at, nk)

    barrier = pltpu.get_barrier_semaphore()

    def greet(device):
        pl.semaphore_signal(barrier, inc=1, device_id=device, device_id_type=MESH)

    def greet_third(d, carry):
        pa, pj = third_peer(d)
        greet((pa, pj, ka))
        return carry

    lax.fori_loop(1, na * nj, greet_third, 0)
    for dk in range(1, nk):
        pk = lax.rem(ka + dk, nk)
        for da in range(na):
            greet((lax.rem(ia + da, na), ja, pk))
        for dj in range(1, nj):
            greet((ia, lax.rem(ja + dj, nj), pk))
    early = min(EARLY, buffers)
    lax.fori_loop(0, early, start_x, 0)
    pl.semaphore_wait(barrier, na * nj - 1 + (nk - 1) * (na + nj - 1))

    def third_copy(d):
        pa, pj = third_peer(d)
        return pltpu.make_async_remote_copy(
            src_ref=third_ref, dst_ref=third_all.at[third_at],
            send_sem=third_send.at[d], recv_sem=third_recv.at[third_at],
            device_id=(pa, pj, ka), device_id_type=MESH,
        )

    def second_copy(d):
        pa, pk = second_peer(d)
        return pltpu.make_async_remote_copy(
            src_ref=second_ref, dst_ref=second_all.at[second_at],
            send_sem=second_send.at[d], recv_sem=second_recv.at[second_at],
            device_id=(pa, ja, pk), device_id_type=MESH,
        )

    def start_third(d, carry):
        third_copy(d).start()
        return carry

    def start_second(d, carry):
        second_copy(d).start()
        return carry

    near[0].wait()
    lax.fori_loop(1, na * nk, start_second, 0)
    near[1].wait()
    lax.fori_loop(1, na * nj, start_third, 0)
    lax.fori_loop(early, buffers, start_x, 0)

    def recv_third(d, carry):
        pa, pj = third_peer(d)
        at = pa * nj + pj
        pltpu.make_async_remote_copy(
            src_ref=third_ref, dst_ref=third_all.at[at],
            send_sem=third_send.at[d], recv_sem=third_recv.at[at],
            device_id=(pa, pj, ka), device_id_type=MESH,
        ).wait_recv()
        return carry

    def recv_second(d, carry):
        pa, pk = second_peer(d)
        at = pa * nk + pk
        pltpu.make_async_remote_copy(
            src_ref=second_ref, dst_ref=second_all.at[at],
            send_sem=second_send.at[d], recv_sem=second_recv.at[at],
            device_id=(pa, ja, pk), device_id_type=MESH,
        ).wait_recv()
        return carry

    def gram3_copy(d, at):
        return pltpu.make_async_remote_copy(
            src_ref=gram3.at[at], dst_ref=gram3.at[at],
            send_sem=gram3_send.at[d], recv_sem=gram3_recv.at[at],
            device_id=(ia, ja, lax.rem(ka + d, nk)), device_id_type=MESH,
        )

    def gram2_copy(d, at):
        return pltpu.make_async_remote_copy(
            src_ref=gram2.at[at], dst_ref=gram2.at[at],
            send_sem=gram2_send.at[d], recv_sem=gram2_recv.at[at],
            device_id=(ia, lax.rem(ja + d, nj), ka), device_id_type=MESH,
        )

    def gram_of(turned):
        pairs = lax.dot_general(
            turned, turned, (((1,), (1,)), ((), ())), preferred_element_type=jnp.float32
        )
        halves = pairs[:rank] + pairs[rank:]
        return halves[:, :rank] + halves[:, rank:]

    lax.fori_loop(1, na * nk, recv_second, 0)
    width = second_hbm.shape[0]
    for s in range(na * nk):
        second_flat[s * width:(s + 1) * width, :] = second_all[s]
    turned2 = jnp.concatenate(split(second_flat[...].T), axis=0)
    weights[...] = jnp.concatenate([turned2, turned2], axis=1)
    gram2[ja] = gram_of(turned2)
    for d in range(1, nj):
        gram2_copy(d, ja).start()

    lax.fori_loop(1, na * nj, recv_third, 0)
    depth = third_hbm.shape[0]
    for s in range(na * nj):
        third_flat[s * depth:(s + 1) * depth, :] = third_all[s]
    third = third_flat[...].T
    scale[...] = jnp.concatenate([third, third], axis=0)
    gram3[ka] = gram_of(jnp.concatenate(split(third), axis=0))
    for d in range(1, nk):
        gram3_copy(d, ka).start()

    inner = x_hbm.shape[2]

    def term_copy(turn):
        owner = owner_at(turn)
        return pltpu.make_async_remote_copy(
            src_ref=terms_out.at[turn], dst_ref=terms_in.at[own],
            send_sem=term_send.at[turn], recv_sem=term_recv.at[own],
            device_id=(ia, owner // nk, lax.rem(owner, nk)), device_id_type=MESH,
        )

    def for_owner(turn, carry):
        slot = lax.rem(turn, buffers)

        @pl.when(turn == n_owner - 1)
        def _():
            near[2].wait()
            for d in range(1, nk):
                gram3_copy(d, lax.rem(ka + d, nk)).wait_recv()
            for d in range(1, nj):
                gram2_copy(d, lax.rem(ja + d, nj)).wait_recv()
            mixed = jnp.sum(gram2[...], axis=0) * jnp.sum(gram3[...], axis=0)
            out_ref[...] = -jnp.dot(
                first_ref[...], mixed, precision=HIGHEST, preferred_element_type=jnp.float32
            )

        x_copy(turn).wait()
        found = []
        for i in range(rows):
            z = jnp.dot(
                weights[...], jnp.concatenate(split(x_buf[slot, i]), axis=0),
                preferred_element_type=jnp.float32,
            )
            z = z * scale[...]
            z = z[:rank] + z[rank:]
            found.append(sum(z[:, at:at + 128] for at in range(0, inner, 128)))
        term = jnp.sum(jnp.stack(found), axis=2)

        @pl.when(turn + buffers < n_owner)
        def _():
            x_copy(turn + buffers).start()

        @pl.when(turn < n_owner - 1)
        def _():
            terms_out[turn] = term
            term_copy(turn).start()

        @pl.when(turn == n_owner - 1)
        def _():
            terms_in[own] = term

        return carry

    lax.fori_loop(0, n_owner, for_owner, 0)

    def recv_term(turn, carry):
        owner = owner_at(turn)
        pltpu.make_async_remote_copy(
            src_ref=terms_out.at[turn], dst_ref=terms_in.at[owner],
            send_sem=term_send.at[turn], recv_sem=term_recv.at[owner],
            device_id=(ia, owner // nk, lax.rem(owner, nk)), device_id_type=MESH,
        ).wait_recv()
        return carry

    lax.fori_loop(0, n_owner - 1, recv_term, 0)
    out_ref[...] += jnp.sum(terms_in[...], axis=0)

    def sent_third(d, carry):
        third_copy(d).wait_send()
        return carry

    def sent_second(d, carry):
        second_copy(d).wait_send()
        return carry

    def sent_term(turn, carry):
        term_copy(turn).wait_send()
        return carry

    lax.fori_loop(1, na * nj, sent_third, 0)
    lax.fori_loop(1, na * nk, sent_second, 0)
    for d in range(1, nk):
        gram3_copy(d, ka).wait_send()
    for d in range(1, nj):
        gram2_copy(d, ja).wait_send()
    lax.fori_loop(0, n_owner - 1, sent_term, 0)


def on_device(na, nj, nk, tensor, first, second, third):
    rows, rank = first.shape
    _, columns, inner = tensor.shape
    buffers = min(BUFFERS, nj * nk)
    dma = pltpu.SemaphoreType.DMA
    f32 = jnp.float32
    vmem = pl.BlockSpec(memory_space=pltpu.VMEM)
    return -pl.pallas_call(
        functools.partial(kernel, na, nj, nk, buffers),
        out_shape=pltpu.VMEM((rows, rank), f32),
        in_specs=[pl.BlockSpec(memory_space=pltpu.HBM)] * 4,
        out_specs=vmem,
        scratch_shapes=[
            pltpu.VMEM(first.shape, f32),
            dma((3,)),
            pltpu.VMEM((buffers, rows, columns, inner), f32),
            dma((buffers,)),
            pltpu.VMEM((na * nj,) + third.shape, f32),
            dma((na * nj,)),
            dma((na * nj,)),
            pltpu.VMEM((na * nk,) + second.shape, f32),
            dma((na * nk,)),
            dma((na * nk,)),
            pltpu.VMEM((inner, rank), f32),
            pltpu.VMEM((columns, rank), f32),
            pltpu.VMEM((2 * rank, 2 * columns), jnp.bfloat16),
            pltpu.VMEM((2 * rank, inner), f32),
            pltpu.VMEM((nk, rank, rank), f32),
            dma((nk,)),
            dma((nk,)),
            pltpu.VMEM((nj, rank, rank), f32),
            dma((nj,)),
            dma((nj,)),
            pltpu.VMEM((nj * nk, rows, rank), f32),
            pltpu.VMEM((nj * nk, rows, rank), f32),
            dma((nj * nk,)),
            dma((nj * nk,)),
        ],
        compiler_params=pltpu.CompilerParams(
            collective_id=0, has_side_effects=True, vmem_limit_bytes=56 * 2**20
        ),
        name="cp_gradient",
    )(tensor, first, second, third)


def solution(mesh):
    sizes = (mesh.shape["ia"], mesh.shape["ja"], mesh.shape["ka"])
    return jax.shard_map(
        functools.partial(on_device, *sizes),
        mesh=mesh,
        in_specs=(
            P("ia", "ja", "ka"),
            P(("ia", "ja", "ka"), None),
            P(("ja", "ia", "ka"), None),
            P(("ka", "ia", "ja"), None),
        ),
        out_specs=P(("ia", "ja", "ka"), None),
        check_vma=False,
    )
```

```python
import functools

import jax
import jax.numpy as jnp
from jax import lax
from jax.experimental import pallas as pl
from jax.experimental.pallas import tpu as pltpu
from jax.sharding import PartitionSpec as P

MESH = pl.DeviceIdType.MESH
HIGHEST = lax.Precision.HIGHEST
BUFFERS = 5
EARLY = 2


def split(x):
    high = x.astype(jnp.bfloat16)
    low = (x - high.astype(jnp.float32)).astype(jnp.bfloat16)
    return high, low


def kernel(
    na, nj, nk, buffers,
    x_hbm, first_hbm, second_hbm, third_hbm, out_ref,
    first_ref, near_sem,
    x_buf, x_sem,
    third_all, third_send, third_recv,
    second_all, second_send, second_recv,
    third_flat, second_flat, weights, scale,
    gram3, gram3_send, gram3_recv,
    gram2, gram2_send, gram2_recv,
    terms_out, terms_in, term_send, term_recv,
):
    ia, ja, ka = lax.axis_index("ia"), lax.axis_index("ja"), lax.axis_index("ka")
    n_owner = nj * nk
    own = ja * nk + ka
    rows = out_ref.shape[0]
    rank = out_ref.shape[1]

    def owner_at(turn):
        return lax.rem(own + 1 + turn, n_owner)

    def x_copy(turn):
        slot = lax.rem(turn, buffers)
        return pltpu.make_async_copy(
            x_hbm.at[pl.ds(owner_at(turn) * rows, rows)], x_buf.at[slot], x_sem.at[slot]
        )

    def start_x(c, carry):
        x_copy(c).start()
        return carry

    third_at = ia * nj + ja
    second_at = ia * nk + ka
    third_ref, second_ref = third_all.at[third_at], second_all.at[second_at]
    near = [
        pltpu.make_async_copy(source, target, near_sem.at[k])
        for k, (source, target) in enumerate(
            [(second_hbm, second_ref), (third_hbm, third_ref), (first_hbm, first_ref)]
        )
    ]
    for copy in near:
        copy.start()

    def third_peer(d):
        at = lax.rem(ia * nj + ja + d, na * nj)
        return at // nj, lax.rem(at, nj)

    def second_peer(d):
        at = lax.rem(ia * nk + ka + d, na * nk)
        return at // nk, lax.rem(at, nk)

    barrier = pltpu.get_barrier_semaphore()

    def greet(device):
        pl.semaphore_signal(barrier, inc=1, device_id=device, device_id_type=MESH)

    def greet_third(d, carry):
        pa, pj = third_peer(d)
        greet((pa, pj, ka))
        return carry

    lax.fori_loop(1, na * nj, greet_third, 0)
    for dk in range(1, nk):
        pk = lax.rem(ka + dk, nk)
        for da in range(na):
            greet((lax.rem(ia + da, na), ja, pk))
        for dj in range(1, nj):
            greet((ia, lax.rem(ja + dj, nj), pk))
    early = min(EARLY, buffers)
    lax.fori_loop(0, early, start_x, 0)
    pl.semaphore_wait(barrier, na * nj - 1 + (nk - 1) * (na + nj - 1))

    def third_copy(d):
        pa, pj = third_peer(d)
        return pltpu.make_async_remote_copy(
            src_ref=third_ref, dst_ref=third_all.at[third_at],
            send_sem=third_send.at[d], recv_sem=third_recv.at[third_at],
            device_id=(pa, pj, ka), device_id_type=MESH,
        )

    def second_copy(d):
        pa, pk = second_peer(d)
        return pltpu.make_async_remote_copy(
            src_ref=second_ref, dst_ref=second_all.at[second_at],
            send_sem=second_send.at[d], recv_sem=second_recv.at[second_at],
            device_id=(pa, ja, pk), device_id_type=MESH,
        )

    def start_third(d, carry):
        third_copy(d).start()
        return carry

    def start_second(d, carry):
        second_copy(d).start()
        return carry

    near[0].wait()
    lax.fori_loop(1, na * nk, start_second, 0)
    near[1].wait()
    lax.fori_loop(1, na * nj, start_third, 0)
    lax.fori_loop(early, buffers, start_x, 0)

    def recv_third(d, carry):
        pa, pj = third_peer(d)
        at = pa * nj + pj
        pltpu.make_async_remote_copy(
            src_ref=third_ref, dst_ref=third_all.at[at],
            send_sem=third_send.at[d], recv_sem=third_recv.at[at],
            device_id=(pa, pj, ka), device_id_type=MESH,
        ).wait_recv()
        return carry

    def recv_second(d, carry):
        pa, pk = second_peer(d)
        at = pa * nk + pk
        pltpu.make_async_remote_copy(
            src_ref=second_ref, dst_ref=second_all.at[at],
            send_sem=second_send.at[d], recv_sem=second_recv.at[at],
            device_id=(pa, ja, pk), device_id_type=MESH,
        ).wait_recv()
        return carry

    def gram3_copy(d, at):
        return pltpu.make_async_remote_copy(
            src_ref=gram3.at[at], dst_ref=gram3.at[at],
            send_sem=gram3_send.at[d], recv_sem=gram3_recv.at[at],
            device_id=(ia, ja, lax.rem(ka + d, nk)), device_id_type=MESH,
        )

    def gram2_copy(d, at):
        return pltpu.make_async_remote_copy(
            src_ref=gram2.at[at], dst_ref=gram2.at[at],
            send_sem=gram2_send.at[d], recv_sem=gram2_recv.at[at],
            device_id=(ia, lax.rem(ja + d, nj), ka), device_id_type=MESH,
        )

    def gram_of(turned):
        pairs = lax.dot_general(
            turned, turned, (((1,), (1,)), ((), ())), preferred_element_type=jnp.float32
        )
        halves = pairs[:rank] + pairs[rank:]
        return halves[:, :rank] + halves[:, rank:]

    lax.fori_loop(1, na * nk, recv_second, 0)
    width = second_hbm.shape[0]
    for s in range(na * nk):
        second_flat[s * width:(s + 1) * width, :] = second_all[s]
    turned2 = jnp.concatenate(split(second_flat[...].T), axis=0)
    weights[...] = jnp.concatenate([turned2, turned2], axis=1)
    gram2[ja] = gram_of(turned2)
    for d in range(1, nj):
        gram2_copy(d, ja).start()

    lax.fori_loop(1, na * nj, recv_third, 0)
    depth = third_hbm.shape[0]
    for s in range(na * nj):
        third_flat[s * depth:(s + 1) * depth, :] = third_all[s]
    third = third_flat[...].T
    scale[...] = third
    gram3[ka] = gram_of(jnp.concatenate(split(third), axis=0))
    for d in range(1, nk):
        gram3_copy(d, ka).start()

    inner = x_hbm.shape[2]

    def term_copy(turn):
        owner = owner_at(turn)
        return pltpu.make_async_remote_copy(
            src_ref=terms_out.at[turn], dst_ref=terms_in.at[own],
            send_sem=term_send.at[turn], recv_sem=term_recv.at[own],
            device_id=(ia, owner // nk, lax.rem(owner, nk)), device_id_type=MESH,
        )

    def for_owner(turn, carry):
        slot = lax.rem(turn, buffers)

        @pl.when(turn == n_owner - 1)
        def _():
            near[2].wait()
            for d in range(1, nk):
                gram3_copy(d, lax.rem(ka + d, nk)).wait_recv()
            for d in range(1, nj):
                gram2_copy(d, lax.rem(ja + d, nj)).wait_recv()
            mixed = jnp.sum(gram2[...], axis=0) * jnp.sum(gram3[...], axis=0)
            out_ref[...] = -jnp.dot(
                first_ref[...], mixed, precision=HIGHEST, preferred_element_type=jnp.float32
            )

        x_copy(turn).wait()
        found = []
        for i in range(rows):
            z = jnp.dot(
                weights[...], jnp.concatenate(split(x_buf[slot, i]), axis=0),
                preferred_element_type=jnp.float32,
            )
            z = (z[:rank] + z[rank:]) * scale[...]
            found.append(sum(z[:, at:at + 128] for at in range(0, inner, 128)))
        term = jnp.sum(jnp.stack(found), axis=2)

        @pl.when(turn + buffers < n_owner)
        def _():
            x_copy(turn + buffers).start()

        @pl.when(turn < n_owner - 1)
        def _():
            terms_out[turn] = term
            term_copy(turn).start()

        @pl.when(turn == n_owner - 1)
        def _():
            terms_in[own] = term

        return carry

    lax.fori_loop(0, n_owner, for_owner, 0)

    def recv_term(turn, carry):
        owner = owner_at(turn)
        pltpu.make_async_remote_copy(
            src_ref=terms_out.at[turn], dst_ref=terms_in.at[owner],
            send_sem=term_send.at[turn], recv_sem=term_recv.at[owner],
            device_id=(ia, owner // nk, lax.rem(owner, nk)), device_id_type=MESH,
        ).wait_recv()
        return carry

    lax.fori_loop(0, n_owner - 1, recv_term, 0)
    out_ref[...] += jnp.sum(terms_in[...], axis=0)

    def sent_third(d, carry):
        third_copy(d).wait_send()
        return carry

    def sent_second(d, carry):
        second_copy(d).wait_send()
        return carry

    def sent_term(turn, carry):
        term_copy(turn).wait_send()
        return carry

    lax.fori_loop(1, na * nj, sent_third, 0)
    lax.fori_loop(1, na * nk, sent_second, 0)
    for d in range(1, nk):
        gram3_copy(d, ka).wait_send()
    for d in range(1, nj):
        gram2_copy(d, ja).wait_send()
    lax.fori_loop(0, n_owner - 1, sent_term, 0)


def on_device(na, nj, nk, tensor, first, second, third):
    rows, rank = first.shape
    _, columns, inner = tensor.shape
    buffers = min(BUFFERS, nj * nk)
    dma = pltpu.SemaphoreType.DMA
    f32 = jnp.float32
    vmem = pl.BlockSpec(memory_space=pltpu.VMEM)
    return -pl.pallas_call(
        functools.partial(kernel, na, nj, nk, buffers),
        out_shape=pltpu.VMEM((rows, rank), f32),
        in_specs=[pl.BlockSpec(memory_space=pltpu.HBM)] * 4,
        out_specs=vmem,
        scratch_shapes=[
            pltpu.VMEM(first.shape, f32),
            dma((3,)),
            pltpu.VMEM((buffers, rows, columns, inner), f32),
            dma((buffers,)),
            pltpu.VMEM((na * nj,) + third.shape, f32),
            dma((na * nj,)),
            dma((na * nj,)),
            pltpu.VMEM((na * nk,) + second.shape, f32),
            dma((na * nk,)),
            dma((na * nk,)),
            pltpu.VMEM((inner, rank), f32),
            pltpu.VMEM((columns, rank), f32),
            pltpu.VMEM((2 * rank, 2 * columns), jnp.bfloat16),
            pltpu.VMEM((rank, inner), f32),
            pltpu.VMEM((nk, rank, rank), f32),
            dma((nk,)),
            dma((nk,)),
            pltpu.VMEM((nj, rank, rank), f32),
            dma((nj,)),
            dma((nj,)),
            pltpu.VMEM((nj * nk, rows, rank), f32),
            pltpu.VMEM((nj * nk, rows, rank), f32),
            dma((nj * nk,)),
            dma((nj * nk,)),
        ],
        compiler_params=pltpu.CompilerParams(
            collective_id=0, has_side_effects=True, vmem_limit_bytes=56 * 2**20
        ),
        name="cp_gradient",
    )(tensor, first, second, third)


def solution(mesh):
    sizes = (mesh.shape["ia"], mesh.shape["ja"], mesh.shape["ka"])
    return jax.shard_map(
        functools.partial(on_device, *sizes),
        mesh=mesh,
        in_specs=(
            P("ia", "ja", "ka"),
            P(("ia", "ja", "ka"), None),
            P(("ja", "ia", "ka"), None),
            P(("ka", "ia", "ja"), None),
        ),
        out_specs=P(("ia", "ja", "ka"), None),
        check_vma=False,
    )
```
